256 devices in a mesh: face: 4 (over z_lo, core), tile: 64 (over y, z_hi, x).
Axes of the slice: x: 4, y: 4, z: 8 (z_hi: 4, z_lo: 2; z = z_hi * 2 + z_lo), core: 2. Of those that a mesh axis runs over, the one named last changes fastest.
Arguments:
- pressure: float32 [64, 4096, 256], P(None, ('face', 'tile')), may hold values from -0.8 to 0.8
- forcing: float32 [64, 4096, 256], P(None, ('face', 'tile')), may hold values from -8 to 8
- stiffness: float32 [64, 4096, 256], P(None, ('face', 'tile')), may hold values from 2 to 8
- vertical_op: float32 [64, 64], replicated, as said below
- col_inverse: float32 [4, 64, 64], replicated, as said below
Outputs:
- updated: float32 [64, 4096, 256], P(None, ('face', 'tile'))
- new_residual: float32 [64, 4096, 256], P(None, ('face', 'tile'))
The draws below stay inside these ranges and needn't reach their ends.
Inputs may be any that keep to these rules, and one draw needn't show every extreme that they name: vertical_op is symmetric positive definite. col_inverse[l] is the float32 inverse of (0.02 + 16 / 4^l) I + vertical_op.
All inputs are finite; a program needn't handle non-finite values.
Results may differ from the reference program's by a relative error of at most 0.0003.
Values sent between devices are 32-bit elements; how exact they have to be, the bound alone decides.
A program may use at most 128 MiB of HBM per device.

```python
import math
import jax
import jax.numpy as jnp
from jax import lax

LEV = 64
CY = 256
LEVELS = 4
COARSE_SWEEPS = 4
NX = 4096


def vertical_pair(key):
    folded = jax.random.fold_in(key, 7)
    coef_key, jitter_key = jax.random.split(folded)
    interfaces = jnp.exp(jax.random.uniform(coef_key, (LEV + 1,), jnp.float32, 0.0, jnp.log(8.0)))
    identity = jnp.eye(LEV, dtype=jnp.float32)
    diag_part = interfaces[:-1] + interfaces[1:] + 0.3
    off_diag = -interfaces[1:-1]
    tridiag = jnp.diag(diag_part) + jnp.diag(off_diag, 1) + jnp.diag(off_diag, -1)
    jitter = jax.random.normal(jitter_key, (LEV, LEV), jnp.float32) * 0.01
    operator = tridiag + (jitter + jitter.T) * 0.7071
    inverses = jnp.stack([jnp.linalg.inv((0.02 + 16.0 / 4.0 ** grid_level) * identity + operator) for grid_level in range(LEVELS)])
    return (operator, inverses)


def draw_vertical_op(key, part):
    return vertical_pair(key)[0]


def draw_col_inverse(key, part):
    return vertical_pair(key)[1]


def steps_of(key, dims, shards, least, largest):
    loudness, own = 1.0, jax.random.fold_in(key, 6)
    for axis_at, shards_of in shards:
        steps = jnp.exp(jax.random.uniform(jax.random.fold_in(own, axis_at), (shards_of,), jnp.float32, least / len(shards), largest / len(shards)))
        loudness = loudness * jnp.repeat(steps, dims[axis_at] // shards_of).reshape([-1 if axis == axis_at else 1 for axis in range(len(dims))])
    return loudness


def bell_draw(rng, extent, width, reach, pieces=(), held_as=jnp.bfloat16):
    drawn = jax.random.normal(rng, extent, jnp.float32) * width
    if len(pieces) > 0:
        drawn = steps_of(rng, extent, pieces, -0.22, 0.18) * drawn
    return jnp.clip(drawn, min=-reach, max=reach).astype(held_as)


def setup_inputs(seed: int = 0) -> dict:
    key_of = jax.random.split(jax.random.key(seed), 6)
    return {
        "pressure": bell_draw(key_of[0], (LEV, NX, CY), 0.1, 0.8, ((1, 256),), jnp.float32),
        "forcing": bell_draw(key_of[1], (LEV, NX, CY), 1.0, 8.0, ((1, 256),), jnp.float32),
        "stiffness": jnp.clip(jnp.exp(math.log(8.0) - 1.3862944 * jax.random.uniform(key_of[2], (LEV, NX, CY), jnp.float32) ** steps_of(key_of[2], (LEV, NX, CY), ((1, 256),), -0.2, 0.2)), 2.0, 8.0),
        "vertical_op": draw_vertical_op(jax.random.fold_in(key_of[5], 71), 0),
        "col_inverse": draw_col_inverse(jax.random.fold_in(key_of[5], 71), 0),
    }


damping = 0.02
relax_weight = 0.6
nominal_stiff = 16.0

def column_apply(matrix, values):
    flattened = values.reshape(values.shape[0], -1)
    return jnp.dot(matrix.astype(jnp.float32), flattened.astype(jnp.float32), precision=lax.Precision.HIGHEST, preferred_element_type=jnp.float32).reshape(values.shape)

def lateral_sum(values):
    zero_col = jnp.zeros_like(values[:, :, :1])
    upward = jnp.concatenate([values[:, :, 1:], zero_col], axis=2)
    downward = jnp.concatenate([zero_col, values[:, :, :-1]], axis=2)
    return upward + downward

def operator_from(values, beside_sum, stiffness, vertical_op):
    horizontal = stiffness * (4.0 * values - beside_sum - lateral_sum(values))
    return damping * values + horizontal + column_apply(vertical_op, values)

def loop_operator(values, stiffness, vertical_op):
    beside_sum = jnp.roll(values, 1, 1) + jnp.roll(values, -1, 1)
    return operator_from(values, beside_sum, stiffness, vertical_op)

def coarsen(values):
    return values.reshape(values.shape[0], values.shape[1] // 2, 2, values.shape[2] // 2, 2).mean(axis=(2, 4))

def refine(values):
    return jnp.repeat(jnp.repeat(values, 2, axis=1), 2, axis=2)

def relax_step(correction, source, scaling, matrix, operator):
    return correction + relax_weight * column_apply(matrix, scaling * (source - operator(correction)))

def vcycle(source, stiffness, vertical_op, col_inverse, grid_level):
    scaling = (damping + nominal_stiff / 4.0 ** grid_level) / (damping + 4.0 * stiffness)
    matrix = col_inverse[grid_level]

    def operator(values):
        return loop_operator(values, stiffness, vertical_op)
    correction = relax_weight * column_apply(matrix, scaling * source)
    if grid_level == LEVELS - 1:
        for sweep_index in range(COARSE_SWEEPS - 1):
            correction = relax_step(correction, source, scaling, matrix, operator)
        return correction
    correction = relax_step(correction, source, scaling, matrix, operator)
    residue = source - operator(correction)
    coarse_fix = vcycle(coarsen(residue), coarsen(stiffness) / 4.0, vertical_op, col_inverse, grid_level + 1)
    correction = correction + refine(coarse_fix)
    for sweep_index in range(2):
        correction = relax_step(correction, source, scaling, matrix, operator)
    return correction

def reference(pressure, forcing, stiffness, vertical_op, col_inverse):
    start_res = forcing - loop_operator(pressure, stiffness, vertical_op)
    updated = pressure + vcycle(start_res, stiffness, vertical_op, col_inverse, 0)
    return (updated, forcing - loop_operator(updated, stiffness, vertical_op))
```

```python
import functools

import jax
import jax.numpy as jnp
from jax import lax
from jax.experimental import pallas as pl
from jax.experimental.pallas import tpu as pltpu
from jax.sharding import PartitionSpec as P

LEVELS = 4
LEV = 64
damping = 0.02
relax_weight = 0.6
nominal_stiff = 16.0
F32, BF16 = jnp.float32, jnp.bfloat16
MESH = pl.DeviceIdType.MESH
LANES = 128

HALO = (4, 4, 4, 5)

MESSAGES = (
    "p", "k", "r", "k_far", "k1", "k2", "k3", "k3_2", "k3_3", "d", "b1", "r0", "b2", "r1", "c1",
    "b3", "b3_2", "b3_3", "r2", "c2",
)


def split(x):
    high = x.astype(BF16)
    return high, (x - high.astype(F32)).astype(BF16)


def rows(lo, hi, step, fn):
    whole, rest = divmod(hi - lo, step)
    if whole > 1:
        def body(i, carry):
            base = lo + i * step
            fn([base + j for j in range(step)])
            return carry
        lax.fori_loop(0, whole, body, 0)
    elif whole == 1:
        fn([lo + j for j in range(step)])
    if rest:
        fn([hi - rest + j for j in range(rest)])


def lateral(x, masked):
    width = x.shape[1]
    below, above = pltpu.roll(x, 1, 1), pltpu.roll(x, width - 1, 1)
    if masked:
        lane = lax.broadcasted_iota(jnp.int32, x.shape, 1)
        below = jnp.where(lane == 0, 0.0, below)
        above = jnp.where(lane == width - 1, 0.0, above)
    return below + above


def kernel(
    faces, tiles, p_hbm, f_hbm, k_hbm, vop_ref, inv_ref, out_u, out_r,
    p0, k0, s0, r0, da0, db0, e0, v0, ph, rh, dh, lr0,
    k1, s1, r1, da1, db1, c1, e1, v1, lr1, lc1,
    k2, s2, r2, da2, db2, c2, e2, v2, lr2, lc2,
    k3, s3, r3, da3, db3, c3, v3, c0,
    w_ref, wv_ref, coarse_ref, coarse0_ref, fine_ref, fine0_ref,
    in_sem, out_sem, send_sem, recv_sem,
):
    count = faces * tiles
    me = lax.axis_index("face") * tiles + lax.axis_index("tile")

    def device(offset):
        other = lax.rem(me + (offset + count), count)
        return (other // tiles, lax.rem(other, tiles))

    barrier = pltpu.get_barrier_semaphore()
    for offset in (-3, -2, -1, 1, 2, 3):
        pl.semaphore_signal(barrier, inc=1, device_id=device(offset), device_id_type=MESH)

    K, S, R, DA, DB = (k0, k1, k2, k3), (s0, s1, s2, s3), (r0, r1, r2, r3), (da0, da1, da2, da3), (db0, db1, db2, db3)
    C = (c0, c1, c2, c3)
    own = tuple(n_rows >> level for level, n_rows in enumerate((16,) * LEVELS))
    H = HALO

    for i in range(16):
        pltpu.make_async_copy(p_hbm.at[:, i, :], p0.at[1 + i], in_sem.at[0]).start()
    for i in range(16):
        pltpu.make_async_copy(k_hbm.at[:, i, :], k0.at[H[0] + i], in_sem.at[1]).start()
    for i in range(16):
        pltpu.make_async_copy(f_hbm.at[:, i, :], r0.at[H[0] + i], in_sem.at[2]).start()

    def beside(m):
        high, low = split(m)
        return jnp.concatenate([high, high, low], axis=1)

    for level in range(LEVELS):
        w_ref[level] = beside(inv_ref[level])
    row, col = (lax.broadcasted_iota(jnp.int32, (LEV, LEV), a) for a in (0, 1))
    wv_ref[...] = beside(vop_ref[...] + jnp.where(row == col, damping, 0.0))

    def pairs(n_in, n_out, fold):
        a, b = (lax.broadcasted_iota(jnp.int32, (2 * n_in, n_out), x) for x in (0, 1))
        a = jnp.where(a >= n_in, a - n_in, a)
        hit = (a // 2 == b) if fold else (a == b // 2)
        return jnp.where(hit, 1.0, 0.0).astype(BF16)

    coarse0_ref[...] = pairs(256, 128, True)
    coarse_ref[...] = pairs(128, 128, True)
    fine0_ref[...] = pairs(128, 256, False)
    fine_ref[...] = pairs(128, 128, False)

    def stacked(x):
        high, low = split(x)
        return jnp.concatenate([high, low, high], axis=0)

    def columns(w, x):
        return jnp.dot(w, stacked(x), preferred_element_type=F32)

    def lanes(x, matrix):
        high, low = split(x)
        return jnp.dot(jnp.concatenate([high, low], axis=1), matrix, preferred_element_type=F32)

    def masked(level):
        return level < 2

    def send(name, src, dst, offset, side):
        at = MESSAGES.index(name)
        return pltpu.make_async_remote_copy(
            src_ref=src, dst_ref=dst, send_sem=send_sem.at[at, side], recv_sem=recv_sem.at[at, side],
            device_id=device(offset), device_id_type=MESH,
        )

    pending = {}

    def exchange(name, src_low, dst_low, src_high, dst_high, distance=1):
        copies = (
            send(name, src_low, dst_high, -distance, 0),
            send(name, src_high, dst_low, distance, 1),
        )
        for copy in copies:
            copy.start()
        pending[name] = copies

    def arrived(*names):
        for name in names:
            for copy in pending[name]:
                copy.wait_recv()

    def sent(*names):
        for name in names:
            for copy in pending.pop(name):
                copy.wait_send()

    def scales(level, lo, hi):
        top = relax_weight * (damping + nominal_stiff / 4.0**level)
        def fn(at):
            for i in at:
                S[level][i] = top / (damping + 4.0 * K[level][i])
        rows(lo, hi, 2, fn)

    def relax(level, lo, hi, d_ref):
        def fn(at):
            for i in at:
                d_ref[i] = columns(w_ref[level], S[level][i] * R[level][i])
        rows(lo, hi, 4, fn)

    def update(level, lo, hi, d_ref):
        shift = nominal_stiff / 4.0**level
        def fn(at):
            for i in at:
                d = d_ref[i]
                beside_sum = d_ref[i - 1] + d_ref[i + 1] + lateral(d, masked(level))
                t = S[level][i] * R[level][i]
                R[level][i] = R[level][i] - t + shift * d + K[level][i] * (beside_sum - 4.0 * d)
        rows(lo, hi, 2, fn)

    def lift(level, lo, hi, e_ref, v_ref):
        def fn(at):
            for i in at:
                e = e_ref[i]
                beside_sum = e_ref[i - 1] + e_ref[i + 1] + lateral(e, masked(level))
                R[level][i] = R[level][i] - v_ref[i] + K[level][i] * (beside_sum - 4.0 * e)
        rows(lo, hi, 2, fn)

    def coarsen(level, src, dst, scale):
        matrix = coarse0_ref if level == 0 else coarse_ref
        def fn(at):
            for j in at:
                fine = H[level] + 2 * j
                dst[H[level + 1] + j] = lanes(scale * (src[fine] + src[fine + 1]), matrix[...])
        rows(0, own[level + 1], 2, fn)

    def refine(level, lo, hi, src, e_ref, v_ref):
        matrix = fine0_ref if level == 0 else fine_ref
        def fn(at):
            for j in at:
                e = src[j]
                to = H[level] + 2 * (j - H[level + 1])
                value = lanes(e, matrix[...])
                product = lanes(columns(wv_ref[...], e), matrix[...])
                for i in (to, to + 1):
                    e_ref[i] = value
                    v_ref[i] = product
        rows(lo, hi, 2, fn)

    zero = jnp.zeros((LEV, 256), F32)
    p0[0] = zero
    p0[17] = zero
    pltpu.make_async_copy(p0.at[pl.ds(1, 16)], p0.at[pl.ds(1, 16)], in_sem.at[0]).wait()
    pltpu.make_async_copy(k0.at[pl.ds(4, 16)], k0.at[pl.ds(4, 16)], in_sem.at[1]).wait()
    pltpu.make_async_copy(r0.at[pl.ds(4, 16)], r0.at[pl.ds(4, 16)], in_sem.at[2]).wait()

    def start(at):
        for i in at:
            x = p0[i + 1]
            beside_sum = p0[i] + p0[i + 2] + lateral(x, True)
            r0[i + 4] = r0[i + 4] - columns(wv_ref[...], x) + k0[i + 4] * (beside_sum - 4.0 * x)
    rows(0, 16, 2, start)
    dh[2] = r0[4]
    dh[3] = r0[19]

    pl.semaphore_wait(barrier, 6)
    exchange("p", p0.at[1], ph.at[0], p0.at[16], ph.at[1])
    exchange("k", k0.at[4], k0.at[3], k0.at[19], k0.at[20])
    exchange("r", dh.at[2], rh.at[0], dh.at[3], rh.at[1])
    exchange("k_far", k0.at[5], k0.at[2], k0.at[18], k0.at[21])

    for level in range(LEVELS - 1):
        coarsen(level, K[level], K[level + 1], 1.0 / 16.0)
    exchange("k1", k1.at[pl.ds(4, 3)], k1.at[pl.ds(1, 3)], k1.at[pl.ds(9, 3)], k1.at[pl.ds(12, 3)])
    exchange("k2", k2.at[pl.ds(4, 3)], k2.at[pl.ds(1, 3)], k2.at[pl.ds(5, 3)], k2.at[pl.ds(8, 3)])
    exchange("k3", k3.at[pl.ds(5, 2)], k3.at[pl.ds(3, 2)], k3.at[pl.ds(5, 2)], k3.at[pl.ds(7, 2)])
    exchange("k3_2", k3.at[pl.ds(5, 2)], k3.at[pl.ds(1, 2)], k3.at[pl.ds(5, 2)], k3.at[pl.ds(9, 2)], 2)
    exchange("k3_3", k3.at[5], k3.at[0], k3.at[6], k3.at[11], 3)

    scales(0, 4, 20)
    relax(0, 5, 19, da0)
    update(0, 6, 18, da0)
    relax(0, 6, 18, db0)
    db0[3] = zero
    db0[20] = zero
    update(0, 7, 17, db0)
    scales(1, 4, 12)
    scales(2, 4, 8)
    scales(3, 5, 7)

    arrived("p", "k", "r")
    for side, edge, halo in ((0, 4, 3), (1, 19, 20)):
        r0[halo] = rh[side] + k0[halo] * p0[edge - 3]
        r0[edge] = r0[edge] + k0[edge] * ph[side]
        scales(0, halo, halo + 1)
    for lo, hi in ((3, 5), (19, 21)):
        relax(0, lo, hi, da0)
    for lo, hi in ((4, 6), (18, 20)):
        update(0, lo, hi, da0)
    for lo, hi in ((4, 6), (18, 20)):
        relax(0, lo, hi, db0)
    exchange("d", db0.at[4], dh.at[0], db0.at[19], dh.at[1])
    for lo, hi in ((4, 7), (17, 20)):
        update(0, lo, hi, db0)
    coarsen(0, r0, r1, 0.25)
    for n, i in enumerate((4, 5, 10, 11)):
        lr1[6 + n] = r1[i]
    for n, i in enumerate((4, 5, 18, 19)):
        lr0[4 + n] = r0[i]
    exchange("b1", lr1.at[pl.ds(6, 2)], r1.at[pl.ds(2, 2)], lr1.at[pl.ds(8, 2)], r1.at[pl.ds(12, 2)])
    exchange("r0", lr0.at[pl.ds(4, 2)], lr0.at[pl.ds(0, 2)], lr0.at[pl.ds(6, 2)], lr0.at[pl.ds(2, 2)])

    def gather(at):
        for i in at:
            c0[i - 4] = p0[i - 3] + da0[i] + db0[i]
    rows(4, 20, 2, gather)
    arrived("k_far", "k1", "k2", "k3", "k3_2", "k3_3")
    for lo, hi in ((2, 3), (21, 22)):
        scales(0, lo, hi)
    for lo, hi in ((1, 4), (12, 15)):
        scales(1, lo, hi)
    for lo, hi in ((1, 4), (8, 11)):
        scales(2, lo, hi)
    for lo, hi in ((0, 5), (7, 12)):
        scales(3, lo, hi)

    arrived("d", "b1")
    for side, edge, halo, edge1, halo1 in ((0, 4, 3, 4, 3), (1, 19, 20, 11, 12)):
        mine = k0[edge] * dh[side]
        theirs = k0[halo] * db0[edge]
        r0[edge] = r0[edge] + mine
        dh[4 + side] = theirs
        r1[edge1] = r1[edge1] + lanes(0.25 * mine, coarse0_ref[...])
        r1[halo1] = r1[halo1] + lanes(0.25 * theirs, coarse0_ref[...])

    relax(1, 2, 14, da1)
    update(1, 3, 13, da1)
    relax(1, 3, 13, db1)
    update(1, 4, 12, db1)
    coarsen(1, r1, r2, 0.25)
    exchange("b2", r2.at[pl.ds(4, 2)], lr2.at[pl.ds(6, 2)], r2.at[pl.ds(6, 2)], lr2.at[pl.ds(8, 2)])
    for i in range(4, 12):
        c1[i] = da1[i] + db1[i]
    exchange("r1", r1.at[pl.ds(4, 3)], lr1.at[pl.ds(0, 3)], r1.at[pl.ds(9, 3)], lr1.at[pl.ds(3, 3)])
    exchange("c1", c1.at[pl.ds(4, 2)], lc1.at[pl.ds(0, 2)], c1.at[pl.ds(10, 2)], lc1.at[pl.ds(2, 2)])

    arrived("r0")
    r0[2] = lr0[0]
    r0[3] = lr0[1] + dh[4]
    r0[20] = lr0[2] + dh[5]
    r0[21] = lr0[3]

    arrived("b2")
    sent("b2")
    for n, i in enumerate((2, 3, 8, 9)):
        r2[i] = lr2[6 + n]
    relax(2, 2, 10, da2)
    update(2, 3, 9, da2)
    relax(2, 3, 9, db2)
    update(2, 4, 8, db2)
    coarsen(2, r2, r3, 0.25)
    for n in range(2):
        lr2[10 + n] = r3[5 + n]
    b3 = lr2.at[pl.ds(10, 2)]
    exchange("b3", b3, r3.at[pl.ds(3, 2)], b3, r3.at[pl.ds(7, 2)])
    exchange("b3_2", b3, r3.at[pl.ds(1, 2)], b3, r3.at[pl.ds(9, 2)], 2)
    exchange("b3_3", lr2.at[10], r3.at[0], lr2.at[11], r3.at[11], 3)
    for i in range(4, 8):
        c2[i] = da2[i] + db2[i]
    exchange("r2", r2.at[pl.ds(4, 3)], lr2.at[pl.ds(0, 3)], r2.at[pl.ds(5, 3)], lr2.at[pl.ds(3, 3)])
    exchange("c2", c2.at[pl.ds(4, 2)], lc2.at[pl.ds(0, 2)], c2.at[pl.ds(6, 2)], lc2.at[pl.ds(2, 2)])

    arrived("b3", "b3_2", "b3_3")
    relax(3, 0, 12, da3)
    update(3, 1, 11, da3)
    relax(3, 1, 11, db3)
    update(3, 2, 10, db3)
    def first(at):
        for i in at:
            c3[i] = da3[i] + db3[i]
    rows(3, 9, 2, first)
    relax(3, 2, 10, da3)
    update(3, 3, 9, da3)
    relax(3, 3, 9, db3)
    def last(at):
        for i in at:
            c3[i] = c3[i] + da3[i] + db3[i]
    rows(3, 9, 2, last)

    refine(2, 3, 9, c3, e2, v2)
    arrived("r2", "c2")
    sent("r2", "c2")
    for n, i in enumerate((1, 2, 3, 8, 9, 10)):
        r2[i] = lr2[n]
    for n, i in enumerate((2, 3, 8, 9)):
        c2[i] = lc2[n]
    lift(2, 1, 11, e2, v2)
    relax(2, 1, 11, da2)
    update(2, 2, 10, da2)
    relax(2, 2, 10, db2)
    def sum2(at):
        for i in at:
            c2[i] = c2[i] + e2[i] + da2[i] + db2[i]
    rows(2, 10, 2, sum2)

    refine(1, 2, 10, c2, e1, v1)
    arrived("r1", "c1")
    sent("r1", "c1")
    for n, i in enumerate((1, 2, 3, 12, 13, 14)):
        r1[i] = lr1[n]
    for n, i in enumerate((2, 3, 12, 13)):
        c1[i] = lc1[n]
    lift(1, 1, 15, e1, v1)
    relax(1, 1, 15, da1)
    update(1, 2, 14, da1)
    relax(1, 2, 14, db1)
    def sum1(at):
        for i in at:
            c1[i] = c1[i] + e1[i] + da1[i] + db1[i]
    rows(2, 14, 2, sum1)

    refine(0, 2, 14, c1, e0, v0)
    sent("d")
    lift(0, 2, 22, e0, v0)
    relax(0, 2, 22, da0)
    update(0, 3, 21, da0)
    relax(0, 3, 21, db0)
    def sum0(at):
        for i in at:
            c0[i - 4] = c0[i - 4] + e0[i] + da0[i] + db0[i]
    rows(4, 20, 2, sum0)
    for i in range(16):
        pltpu.make_async_copy(c0.at[i], out_u.at[:, i, :], out_sem.at[0]).start()
    update(0, 4, 20, db0)
    for i in range(16):
        pltpu.make_async_copy(r0.at[4 + i], out_r.at[:, i, :], out_sem.at[1]).start()
    sent(*list(pending))
    pltpu.make_async_copy(c0, c0, out_sem.at[0]).wait()
    pltpu.make_async_copy(r0.at[pl.ds(4, 16)], r0.at[pl.ds(4, 16)], out_sem.at[1]).wait()


def solution(mesh):
    faces, tiles = mesh.shape["face"], mesh.shape["tile"]

    def field(count, width):
        return pltpu.VMEM((count, LEV, width), F32)

    def body(pressure, forcing, stiffness, vertical_op, col_inverse):
        out = jax.ShapeDtypeStruct(pressure.shape, F32)
        def level(n, extra):
            return [field(n, LANES)] * 8 + [field(m, LANES) for m in extra]
        scratch = (
            [field(18, 256)] + [field(24, 256)] * 7 + [field(2, 256)] * 2 + [field(6, 256), field(8, 256)]
            + level(16, (10, 4)) + level(12, (12, 4))
            + [field(12, LANES)] * 6 + [field(12, LANES), field(16, 256)]
            + [
                pltpu.VMEM((LEVELS, LEV, 3 * LEV), BF16),
                pltpu.VMEM((LEV, 3 * LEV), BF16),
                pltpu.VMEM((256, 128), BF16),
                pltpu.VMEM((512, 128), BF16),
                pltpu.VMEM((256, 128), BF16),
                pltpu.VMEM((256, 256), BF16),
                pltpu.SemaphoreType.DMA((3,)),
                pltpu.SemaphoreType.DMA((2,)),
                pltpu.SemaphoreType.DMA((len(MESSAGES), 2)),
                pltpu.SemaphoreType.DMA((len(MESSAGES), 2)),
            ]
        )
        return pl.pallas_call(
            functools.partial(kernel, faces, tiles),
            out_shape=(out, out),
            in_specs=[pl.BlockSpec(memory_space=pl.ANY)] * 3 + [pl.BlockSpec(memory_space=pltpu.VMEM)] * 2,
            out_specs=(pl.BlockSpec(memory_space=pl.ANY),) * 2,
            scratch_shapes=scratch,
            compiler_params=pltpu.CompilerParams(
                collective_id=0, has_side_effects=True, vmem_limit_bytes=48 * 1024 * 1024
            ),
            cost_estimate=pl.CostEstimate(flops=2_000_000_000, bytes_accessed=5_000_000, transcendentals=0),
        )(pressure, forcing, stiffness, vertical_op, col_inverse)

    belt = P(None, ("face", "tile"), None)
    return jax.shard_map(
        body,
        mesh=mesh,
        in_specs=(belt, belt, belt, P(), P()),
        out_specs=(belt, belt),
        check_vma=False,
    )
```

```python
import functools

import jax
import jax.numpy as jnp
from jax import lax
from jax.experimental import pallas as pl
from jax.experimental.pallas import tpu as pltpu
from jax.sharding import PartitionSpec as P

LEVELS = 4
LEV = 64
damping = 0.02
relax_weight = 0.6
nominal_stiff = 16.0
F32, BF16 = jnp.float32, jnp.bfloat16
MESH = pl.DeviceIdType.MESH
LANES = 128
VMEM_MIB = 62

HALO = (4, 4, 4, 5)

MESSAGES = (
    "p", "k", "r", "k_far", "k1", "k2", "k3", "k3_2", "k3_3", "d", "b1", "r0", "b2", "r1", "c1",
    "b3", "b3_2", "b3_3", "r2",
)


def split(x):
    high = x.astype(BF16)
    return high, (x - high.astype(F32)).astype(BF16)


def rows(lo, hi, step, fn):
    whole, rest = divmod(hi - lo, step)
    if whole > 1:
        def body(i, carry):
            base = lo + i * step
            fn([base + j for j in range(step)])
            return carry
        lax.fori_loop(0, whole, body, 0)
    elif whole == 1:
        fn([lo + j for j in range(step)])
    if rest:
        fn([hi - rest + j for j in range(rest)])


def lateral(x, masked):
    width = x.shape[1]
    below, above = pltpu.roll(x, 1, 1), pltpu.roll(x, width - 1, 1)
    if masked:
        lane = lax.broadcasted_iota(jnp.int32, x.shape, 1)
        below = jnp.where(lane == 0, 0.0, below)
        above = jnp.where(lane == width - 1, 0.0, above)
    return below + above


def kernel(
    faces, tiles, p_hbm, f_hbm, k_hbm, vop_ref, inv_ref, out_u, out_r,
    p0, k0, s0, r0, da0, db0, e0, v0, ph, rh, dh, lr0,
    k1, s1, r1, da1, db1, c1, e1, v1, lr1, lc1,
    k2, s2, r2, da2, db2, c2, e2, v2, lr2, lb2,
    k3, s3, r3, da3, db3, c3, c0, lk2, q2, q3, lq3,
    w_ref, wv_ref, coarse_ref, coarse0_ref, fine_ref, fine0_ref,
    in_sem, out_sem, send_sem, recv_sem,
):
    count = faces * tiles
    me = lax.axis_index("face") * tiles + lax.axis_index("tile")

    def device(offset):
        other = lax.rem(me + (offset + count), count)
        return (other // tiles, lax.rem(other, tiles))

    barrier = pltpu.get_barrier_semaphore()
    for offset in (-3, -2, -1, 1, 2, 3):
        pl.semaphore_signal(barrier, inc=1, device_id=device(offset), device_id_type=MESH)

    K, S, R, DA, DB = (k0, k1, k2, k3), (s0, s1, s2, s3), (r0, r1, r2, r3), (da0, da1, da2, da3), (db0, db1, db2, db3)
    C = (c0, c1, c2, c3)
    own = tuple(n_rows >> level for level, n_rows in enumerate((16,) * LEVELS))
    H = HALO

    for i in range(16):
        pltpu.make_async_copy(p_hbm.at[:, i, :], p0.at[1 + i], in_sem.at[0]).start()
    for i in range(16):
        pltpu.make_async_copy(k_hbm.at[:, i, :], k0.at[H[0] + i], in_sem.at[1]).start()
    for i in range(16):
        pltpu.make_async_copy(f_hbm.at[:, i, :], r0.at[H[0] + i], in_sem.at[2]).start()

    def beside(m):
        high, low = split(m)
        return jnp.concatenate([high, high, low], axis=1)

    for level in range(LEVELS):
        w_ref[level] = beside(inv_ref[level])
    row, col = (lax.broadcasted_iota(jnp.int32, (LEV, LEV), a) for a in (0, 1))
    wv_ref[...] = beside(vop_ref[...] + jnp.where(row == col, damping, 0.0))

    def pairs(n_in, n_out, fold):
        a, b = (lax.broadcasted_iota(jnp.int32, (2 * n_in, n_out), x) for x in (0, 1))
        a = jnp.where(a >= n_in, a - n_in, a)
        hit = (a // 2 == b) if fold else (a == b // 2)
        return jnp.where(hit, 1.0, 0.0).astype(BF16)

    coarse0_ref[...] = pairs(256, 128, True)
    coarse_ref[...] = pairs(128, 128, True)
    fine0_ref[...] = pairs(128, 256, False)
    fine_ref[...] = pairs(128, 128, False)

    def stacked(x):
        high, low = split(x)
        return jnp.concatenate([high, low, high], axis=0)

    def columns(w, x):
        return jnp.dot(w, stacked(x), preferred_element_type=F32)

    def lanes(x, matrix):
        high, low = split(x)
        return jnp.dot(jnp.concatenate([high, low], axis=1), matrix, preferred_element_type=F32)

    def lane_mask(x, lo, hi):
        lane = lax.broadcasted_iota(jnp.int32, x.shape, 1)
        return jnp.where((lane >= lo) & (lane < hi), x, 0.0)

    def pack2(a, b):
        return a + pltpu.roll(b, 64, 1)

    def unpack2(x):
        return lane_mask(x, 0, 64), lane_mask(pltpu.roll(x, 64, 1), 0, 64)

    def pack3(a, b):
        both = a + pltpu.roll(b, 32, 1)
        half = LEV // 2
        return both[:half] + pltpu.roll(both[half:], 64, 1)

    def unpack3(x):
        parts = [x] + [pltpu.roll(x, shift, 1) for shift in (64, 96, 32)]
        parts = [lane_mask(part, 0, 32) for part in parts]
        return jnp.concatenate(parts[:2], axis=0), jnp.concatenate(parts[2:], axis=0)

    def spread3(name, at):
        for distance in (1, 2, 3):
            low, high = at * 6 + 3 - distance, at * 6 + 2 + distance
            suffix = "" if distance == 1 else "_%d" % distance
            exchange(name + suffix, q3.at[at], lq3.at[low], q3.at[at], lq3.at[high], distance)

    def gather3(at, to):
        for n, i in enumerate((-1, 1, 3, 7, 9, 11)):
            first_row, second_row = unpack3(lq3[at * 6 + n])
            if i >= 0:
                to[i] = first_row
            if i + 1 < 12:
                to[i + 1] = second_row

    def masked(level):
        return level < 2

    def send(name, src, dst, offset, side):
        at = MESSAGES.index(name)
        return pltpu.make_async_remote_copy(
            src_ref=src, dst_ref=dst, send_sem=send_sem.at[at, side], recv_sem=recv_sem.at[at, side],
            device_id=device(offset), device_id_type=MESH,
        )

    pending = {}

    def exchange(name, src_low, dst_low, src_high, dst_high, distance=1):
        copies = (
            send(name, src_low, dst_high, -distance, 0),
            send(name, src_high, dst_low, distance, 1),
        )
        for copy in copies:
            copy.start()
        pending[name] = copies

    def arrived(*names):
        for name in names:
            for copy in pending[name]:
                copy.wait_recv()

    def sent(*names):
        for name in names:
            for copy in pending.pop(name):
                copy.wait_send()

    def scales(level, lo, hi):
        top = relax_weight * (damping + nominal_stiff / 4.0**level)
        def fn(at):
            for i in at:
                S[level][i] = top / (damping + 4.0 * K[level][i])
        rows(lo, hi, 24, fn)

    def relax(level, lo, hi, d_ref):
        def fn(at):
            for i in at:
                d_ref[i] = columns(w_ref[level], S[level][i] * R[level][i])
        rows(lo, hi, 24, fn)

    def update(level, lo, hi, d_ref):
        shift = nominal_stiff / 4.0**level
        def fn(at):
            for i in at:
                d = d_ref[i]
                beside_sum = d_ref[i - 1] + d_ref[i + 1] + lateral(d, masked(level))
                t = S[level][i] * R[level][i]
                R[level][i] = R[level][i] - t + shift * d + K[level][i] * (beside_sum - 4.0 * d)
        rows(lo, hi, 24, fn)

    def lift(level, lo, hi, e_ref, v_ref):
        def fn(at):
            for i in at:
                e = e_ref[i]
                beside_sum = e_ref[i - 1] + e_ref[i + 1] + lateral(e, masked(level))
                R[level][i] = R[level][i] - v_ref[i] + K[level][i] * (beside_sum - 4.0 * e)
        rows(lo, hi, 24, fn)

    def coarsen(level, src, dst, scale, which=None):
        matrix = coarse0_ref if level == 0 else coarse_ref
        def fn(at):
            for j in at:
                fine = H[level] + 2 * j
                dst[H[level + 1] + j] = lanes(scale * (src[fine] + src[fine + 1]), matrix[...])
        fn(range(own[level + 1]) if which is None else which)

    def refine(level, lo, hi, src, e_ref, v_ref):
        matrix = fine0_ref if level == 0 else fine_ref
        def fn(at):
            for j in at:
                e = src[j]
                to = H[level] + 2 * (j - H[level + 1])
                value = lanes(e, matrix[...])
                product = lanes(columns(wv_ref[...], e), matrix[...])
                for i in (to, to + 1):
                    e_ref[i] = value
                    v_ref[i] = product
        rows(lo, hi, 24, fn)

    zero = jnp.zeros((LEV, 256), F32)
    p0[0] = zero
    p0[17] = zero
    pltpu.make_async_copy(p0.at[pl.ds(1, 16)], p0.at[pl.ds(1, 16)], in_sem.at[0]).wait()
    pltpu.make_async_copy(k0.at[pl.ds(4, 16)], k0.at[pl.ds(4, 16)], in_sem.at[1]).wait()
    pltpu.make_async_copy(r0.at[pl.ds(4, 16)], r0.at[pl.ds(4, 16)], in_sem.at[2]).wait()

    def start(at):
        for i in at:
            x = p0[i + 1]
            beside_sum = p0[i] + p0[i + 2] + lateral(x, True)
            r0[i + 4] = r0[i + 4] - columns(wv_ref[...], x) + k0[i + 4] * (beside_sum - 4.0 * x)
    rows(0, 16, 24, start)
    dh[2] = r0[4]
    dh[3] = r0[19]

    pl.semaphore_wait(barrier, 6)
    exchange("p", p0.at[1], ph.at[0], p0.at[16], ph.at[1])
    exchange("k", k0.at[4], k0.at[3], k0.at[19], k0.at[20])
    exchange("r", dh.at[2], rh.at[0], dh.at[3], rh.at[1])

    for level in range(LEVELS - 1):
        coarsen(level, K[level], K[level + 1], 1.0 / 16.0)
    exchange("k1", k1.at[pl.ds(4, 3)], k1.at[pl.ds(1, 3)], k1.at[pl.ds(9, 3)], k1.at[pl.ds(12, 3)])
    q2[6] = pack2(k2[4], k2[5])
    q2[7] = pack2(k2[6], k2[7])
    exchange("k2", q2.at[pl.ds(6, 2)], lk2.at[pl.ds(0, 2)], q2.at[pl.ds(6, 2)], lk2.at[pl.ds(2, 2)])
    q3[0] = pack3(k3[5], k3[6])

    scales(0, 4, 20)
    relax(0, 5, 19, da0)
    update(0, 6, 18, da0)
    relax(0, 6, 18, db0)
    db0[3] = zero
    db0[20] = zero
    update(0, 7, 17, db0)
    coarsen(0, r0, r1, 0.25, (2, 3, 4, 5))
    scales(1, 4, 12)
    scales(2, 4, 8)
    scales(3, 5, 7)

    arrived("p", "k", "r")
    for side, edge, halo in ((0, 4, 3), (1, 19, 20)):
        r0[halo] = rh[side] + k0[halo] * p0[edge - 3]
        r0[edge] = r0[edge] + k0[edge] * ph[side]
        scales(0, halo, halo + 1)
    for lo, hi in ((3, 5), (19, 21)):
        relax(0, lo, hi, da0)
    for lo, hi in ((4, 6), (18, 20)):
        update(0, lo, hi, da0)
    for lo, hi in ((4, 6), (18, 20)):
        relax(0, lo, hi, db0)
    exchange("d", db0.at[4], dh.at[0], db0.at[19], dh.at[1])
    for lo, hi in ((4, 7), (17, 20)):
        update(0, lo, hi, db0)
    coarsen(0, r0, r1, 0.25, (0, 1, 6, 7))
    for n, i in enumerate((4, 5, 10, 11)):
        lr1[6 + n] = r1[i]
    for n, i in enumerate((4, 5, 18, 19)):
        lr0[4 + n] = r0[i]
    exchange("b1", lr1.at[pl.ds(6, 2)], r1.at[pl.ds(2, 2)], lr1.at[pl.ds(8, 2)], r1.at[pl.ds(12, 2)])
    exchange("r0", lr0.at[pl.ds(4, 2)], lr0.at[pl.ds(0, 2)], lr0.at[pl.ds(6, 2)], lr0.at[pl.ds(2, 2)])

    spread3("k3", 0)

    def gather(at):
        for i in at:
            c0[i - 4] = p0[i - 3] + da0[i] + db0[i]
    rows(4, 20, 24, gather)
    arrived("k1", "k2")
    for n in range(4):
        k2[(0, 2, 8, 10)[n]], k2[(1, 3, 9, 11)[n]] = unpack2(lk2[n])
    for lo, hi in ((1, 4), (12, 15)):
        scales(1, lo, hi)
    for lo, hi in ((1, 4), (8, 11)):
        scales(2, lo, hi)

    arrived("d", "b1")
    for side, edge, halo, edge1, halo1 in ((0, 4, 3, 4, 3), (1, 19, 20, 11, 12)):
        mine = k0[edge] * dh[side]
        theirs = k0[halo] * db0[edge]
        r0[edge] = r0[edge] + mine
        dh[4 + side] = theirs
        r1[edge1] = r1[edge1] + lanes(0.25 * mine, coarse0_ref[...])
        r1[halo1] = r1[halo1] + lanes(0.25 * theirs, coarse0_ref[...])

    relax(1, 2, 14, da1)
    update(1, 3, 13, da1)
    relax(1, 3, 13, db1)
    update(1, 4, 12, db1)
    coarsen(1, r1, r2, 0.25)
    q2[4] = pack2(r2[4], r2[5])
    q2[5] = pack2(r2[6], r2[7])
    exchange("b2", q2.at[4], lb2.at[0], q2.at[5], lb2.at[1])
    for i in range(4, 12):
        c1[i] = da1[i] + db1[i]
    exchange("r1", r1.at[pl.ds(4, 3)], lr1.at[pl.ds(0, 3)], r1.at[pl.ds(9, 3)], lr1.at[pl.ds(3, 3)])
    exchange("c1", c1.at[pl.ds(4, 2)], lc1.at[pl.ds(0, 2)], c1.at[pl.ds(10, 2)], lc1.at[pl.ds(2, 2)])

    exchange("k_far", k0.at[5], k0.at[2], k0.at[18], k0.at[21])

    arrived("r0")
    r0[2] = lr0[0]
    r0[3] = lr0[1] + dh[4]
    r0[20] = lr0[2] + dh[5]
    r0[21] = lr0[3]

    arrived("b2")
    r2[2], r2[3] = unpack2(lb2[0])
    r2[8], r2[9] = unpack2(lb2[1])
    relax(2, 2, 10, da2)
    update(2, 3, 9, da2)
    relax(2, 3, 9, db2)
    update(2, 4, 8, db2)
    coarsen(2, r2, r3, 0.25)
    q3[1] = pack3(r3[5], r3[6])
    spread3("b3", 1)
    for i in range(4, 8):
        c2[i] = da2[i] + db2[i]
    q2[0] = pack2(c2[4], c2[5])
    q2[1] = pack2(r2[4], r2[5])
    q2[2] = pack2(r2[6], r2[7])
    q2[3] = pack2(c2[6], c2[7])
    exchange("r2", q2.at[pl.ds(0, 3)], lr2.at[pl.ds(0, 3)], q2.at[pl.ds(1, 3)], lr2.at[pl.ds(3, 3)])
    arrived("k3", "k3_2", "k3_3")
    gather3(0, k3)
    for lo, hi in ((0, 5), (7, 12)):
        scales(3, lo, hi)

    arrived("b3", "b3_2", "b3_3")
    gather3(1, r3)
    relax(3, 0, 12, da3)
    update(3, 1, 11, da3)
    relax(3, 1, 11, db3)
    update(3, 2, 10, db3)
    def first(at):
        for i in at:
            c3[i] = da3[i] + db3[i]
    rows(3, 9, 24, first)
    relax(3, 2, 10, da3)
    update(3, 3, 9, da3)
    relax(3, 3, 9, db3)
    def last(at):
        for i in at:
            c3[i] = c3[i] + da3[i] + db3[i]
    rows(3, 9, 24, last)

    refine(2, 3, 9, c3, e2, v2)
    arrived("r2")
    for n in range(2):
        r2[2 * n], r2[2 * n + 1] = unpack2(lr2[n])
        r2[2 * n + 8], r2[2 * n + 9] = unpack2(lr2[4 + n])
    c2[2], c2[3] = unpack2(lr2[2])
    c2[8], c2[9] = unpack2(lr2[3])
    lift(2, 1, 11, e2, v2)
    relax(2, 1, 11, da2)
    update(2, 2, 10, da2)
    relax(2, 2, 10, db2)
    def sum2(at):
        for i in at:
            c2[i] = c2[i] + e2[i] + da2[i] + db2[i]
    rows(2, 10, 24, sum2)

    refine(1, 2, 10, c2, e1, v1)
    arrived("r1", "c1")
    sent("r1", "c1")
    for n, i in enumerate((1, 2, 3, 12, 13, 14)):
        r1[i] = lr1[n]
    for n, i in enumerate((2, 3, 12, 13)):
        c1[i] = lc1[n]
    lift(1, 1, 15, e1, v1)
    relax(1, 1, 15, da1)
    update(1, 2, 14, da1)
    relax(1, 2, 14, db1)
    def sum1(at):
        for i in at:
            c1[i] = c1[i] + e1[i] + da1[i] + db1[i]
    rows(2, 14, 24, sum1)

    arrived("k_far")
    for lo, hi in ((2, 3), (21, 22)):
        scales(0, lo, hi)
    refine(0, 2, 14, c1, e0, v0)
    sent("d")
    lift(0, 2, 22, e0, v0)
    relax(0, 2, 22, da0)
    update(0, 3, 21, da0)
    relax(0, 3, 21, db0)
    def sum0(at):
        for i in at:
            c0[i - 4] = c0[i - 4] + e0[i] + da0[i] + db0[i]
    rows(4, 20, 24, sum0)
    for i in range(16):
        pltpu.make_async_copy(c0.at[i], out_u.at[:, i, :], out_sem.at[0]).start()
    update(0, 4, 20, db0)
    for i in range(16):
        pltpu.make_async_copy(r0.at[4 + i], out_r.at[:, i, :], out_sem.at[1]).start()
    sent(*list(pending))
    pltpu.make_async_copy(c0, c0, out_sem.at[0]).wait()
    pltpu.make_async_copy(r0.at[pl.ds(4, 16)], r0.at[pl.ds(4, 16)], out_sem.at[1]).wait()


def solution(mesh):
    faces, tiles = mesh.shape["face"], mesh.shape["tile"]

    def field(count, width):
        return pltpu.VMEM((count, LEV, width), F32)

    def body(pressure, forcing, stiffness, vertical_op, col_inverse):
        out = jax.ShapeDtypeStruct(pressure.shape, F32)
        def level(n, extra):
            return [field(n, LANES)] * 8 + [field(m, LANES) for m in extra]
        scratch = (
            [field(18, 256)] + [field(24, 256)] * 7 + [field(2, 256)] * 2 + [field(6, 256), field(8, 256)]
            + level(16, (10, 4)) + level(12, (6, 2))
            + [field(12, LANES)] * 6 + [field(16, 256), field(4, LANES), field(8, LANES)]
            + [pltpu.VMEM((2, LEV // 2, LANES), F32), pltpu.VMEM((12, LEV // 2, LANES), F32)]
            + [
                pltpu.VMEM((LEVELS, LEV, 3 * LEV), BF16),
                pltpu.VMEM((LEV, 3 * LEV), BF16),
                pltpu.VMEM((256, 128), BF16),
                pltpu.VMEM((512, 128), BF16),
                pltpu.VMEM((256, 128), BF16),
                pltpu.VMEM((256, 256), BF16),
                pltpu.SemaphoreType.DMA((3,)),
                pltpu.SemaphoreType.DMA((2,)),
                pltpu.SemaphoreType.DMA((len(MESSAGES), 2)),
                pltpu.SemaphoreType.DMA((len(MESSAGES), 2)),
            ]
        )
        return pl.pallas_call(
            functools.partial(kernel, faces, tiles),
            out_shape=(out, out),
            in_specs=[pl.BlockSpec(memory_space=pl.ANY)] * 3 + [pl.BlockSpec(memory_space=pltpu.VMEM)] * 2,
            out_specs=(pl.BlockSpec(memory_space=pl.ANY),) * 2,
            scratch_shapes=scratch,
            compiler_params=pltpu.CompilerParams(
                collective_id=0, has_side_effects=True, vmem_limit_bytes=VMEM_MIB * 1024 * 1024
            ),
            cost_estimate=pl.CostEstimate(flops=2_000_000_000, bytes_accessed=5_000_000, transcendentals=0),
        )(pressure, forcing, stiffness, vertical_op, col_inverse)

    belt = P(None, ("face", "tile"), None)
    return jax.shard_map(
        body,
        mesh=mesh,
        in_specs=(belt, belt, belt, P(), P()),
        out_specs=(belt, belt),
        check_vma=False,
    )
```

```python
import functools

import jax
import jax.numpy as jnp
from jax import lax
from jax.experimental import pallas as pl
from jax.experimental.pallas import tpu as pltpu
from jax.sharding import PartitionSpec as P

LEVELS = 4
LEV = 64
damping = 0.02
relax_weight = 0.6
nominal_stiff = 16.0
F32, BF16 = jnp.float32, jnp.bfloat16
MESH = pl.DeviceIdType.MESH
LANES = 128
VMEM_MIB = 62

HALO = (4, 4, 4, 5)

MESSAGES = (
    "p", "k", "r", "k_far", "k1", "k2", "k3", "k3_2", "k3_3", "d", "b1", "r0", "b2", "r1", "c1",
    "b3", "b3_2", "b3_3", "r2",
)


def split(x):
    high = x.astype(BF16)
    return high, (x - high.astype(F32)).astype(BF16)


def rows(lo, hi, step, fn):
    whole, rest = divmod(hi - lo, step)
    if whole > 1:
        def body(i, carry):
            base = lo + i * step
            fn([base + j for j in range(step)])
            return carry
        lax.fori_loop(0, whole, body, 0)
    elif whole == 1:
        fn([lo + j for j in range(step)])
    if rest:
        fn([hi - rest + j for j in range(rest)])


def lateral(x, masked):
    width = x.shape[1]
    below, above = pltpu.roll(x, 1, 1), pltpu.roll(x, width - 1, 1)
    if masked:
        lane = lax.broadcasted_iota(jnp.int32, x.shape, 1)
        below = jnp.where(lane == 0, 0.0, below)
        above = jnp.where(lane == width - 1, 0.0, above)
    return below + above


def kernel(
    faces, tiles, p_hbm, f_hbm, k_hbm, vop_ref, inv_ref, out_u, out_r,
    p0, k0, s0, r0, da0, db0, e0, v0, ph, rh, dh, lr0,
    k1, s1, r1, da1, db1, c1, e1, v1, lr1, lc1,
    k2, s2, r2, da2, db2, c2, e2, v2, lr2, lb2,
    k3, s3, r3, da3, db3, c3, c0, lk2, q2, q3, lq3, q4,
    w_ref, wv_ref, coarse_ref, coarse0_ref, fine_ref, fine0_ref,
    in_sem, out_sem, send_sem, recv_sem,
):
    count = faces * tiles
    me = lax.axis_index("face") * tiles + lax.axis_index("tile")

    def device(offset):
        other = lax.rem(me + (offset + count), count)
        return (other // tiles, lax.rem(other, tiles))

    barrier = pltpu.get_barrier_semaphore()
    for offset in (-3, -2, -1, 1, 2, 3):
        pl.semaphore_signal(barrier, inc=1, device_id=device(offset), device_id_type=MESH)

    K, S, R, DA, DB = (k0, k1, k2, k3), (s0, s1, s2, s3), (r0, r1, r2, r3), (da0, da1, da2, da3), (db0, db1, db2, db3)
    C = (c0, c1, c2, c3)
    own = tuple(n_rows >> level for level, n_rows in enumerate((16,) * LEVELS))
    H = HALO

    for i in range(16):
        pltpu.make_async_copy(p_hbm.at[:, i, :], p0.at[1 + i], in_sem.at[0]).start()
    for i in range(16):
        pltpu.make_async_copy(k_hbm.at[:, i, :], k0.at[H[0] + i], in_sem.at[1]).start()
    for i in range(16):
        pltpu.make_async_copy(f_hbm.at[:, i, :], r0.at[H[0] + i], in_sem.at[2]).start()

    def beside(m):
        high, low = split(m)
        return jnp.concatenate([high, high, low], axis=1)

    for level in range(LEVELS):
        w_ref[level] = beside(inv_ref[level])
    row, col = (lax.broadcasted_iota(jnp.int32, (LEV, LEV), a) for a in (0, 1))
    wv_ref[...] = beside(vop_ref[...] + jnp.where(row == col, damping, 0.0))

    def pairs(n_in, n_out, fold):
        a, b = (lax.broadcasted_iota(jnp.int32, (2 * n_in, n_out), x) for x in (0, 1))
        a = jnp.where(a >= n_in, a - n_in, a)
        hit = (a // 2 == b) if fold else (a == b // 2)
        return jnp.where(hit, 1.0, 0.0).astype(BF16)

    coarse0_ref[...] = pairs(256, 128, True)
    coarse_ref[...] = pairs(128, 128, True)
    fine0_ref[...] = pairs(128, 256, False)
    fine_ref[...] = pairs(128, 128, False)

    def stacked(x):
        high, low = split(x)
        return jnp.concatenate([high, low, high], axis=0)

    def columns(w, x):
        return jnp.dot(w, stacked(x), preferred_element_type=F32)

    def lanes(x, matrix):
        high, low = split(x)
        return jnp.dot(jnp.concatenate([high, low], axis=1), matrix, preferred_element_type=F32)

    def lane_mask(x, lo, hi):
        lane = lax.broadcasted_iota(jnp.int32, x.shape, 1)
        return jnp.where((lane >= lo) & (lane < hi), x, 0.0)

    def pack2(a, b):
        return a + pltpu.roll(b, 64, 1)

    def unpack2(x):
        return lane_mask(x, 0, 64), lane_mask(pltpu.roll(x, 64, 1), 0, 64)

    def pack3(a, b):
        both = a + pltpu.roll(b, 32, 1)
        half = LEV // 2
        return both[:half] + pltpu.roll(both[half:], 64, 1)

    def unpack3(x):
        parts = [x] + [pltpu.roll(x, shift, 1) for shift in (64, 96, 32)]
        parts = [lane_mask(part, 0, 32) for part in parts]
        return jnp.concatenate(parts[:2], axis=0), jnp.concatenate(parts[2:], axis=0)

    def pack4(x):
        quarter = LEV // 4
        parts = [x[n * quarter : (n + 1) * quarter] for n in range(4)]
        return sum(pltpu.roll(part, 32 * n, 1) for n, part in enumerate(parts[1:], 1)) + parts[0]

    def unpack4(x):
        parts = [x] + [pltpu.roll(x, LANES - 32 * n, 1) for n in (1, 2, 3)]
        return jnp.concatenate([lane_mask(part, 0, 32) for part in parts], axis=0)

    def spread3(name, at, src):
        q3[at] = pack3(src[5], src[6])
        q4[2 * at] = pack4(src[5])
        q4[2 * at + 1] = pack4(src[6])
        for distance in (1, 2):
            low, high = at * 6 + 3 - distance, at * 6 + 2 + distance
            suffix = "" if distance == 1 else "_%d" % distance
            exchange(name + suffix, q3.at[at], lq3.at[low], q3.at[at], lq3.at[high], distance)
        first_in, last_in = 4 + 2 * at, 5 + 2 * at
        exchange(name + "_3", q4.at[2 * at], q4.at[first_in], q4.at[2 * at + 1], q4.at[last_in], 3)

    def gather3(at, to):
        for n, i in ((1, 1), (2, 3), (3, 7), (4, 9)):
            to[i], to[i + 1] = unpack3(lq3[at * 6 + n])
        to[0] = unpack4(q4[4 + 2 * at])
        to[11] = unpack4(q4[5 + 2 * at])

    def masked(level):
        return level < 2

    def send(name, src, dst, offset, side):
        at = MESSAGES.index(name)
        return pltpu.make_async_remote_copy(
            src_ref=src, dst_ref=dst, send_sem=send_sem.at[at, side], recv_sem=recv_sem.at[at, side],
            device_id=device(offset), device_id_type=MESH,
        )

    pending = {}

    def exchange(name, src_low, dst_low, src_high, dst_high, distance=1):
        copies = (
            send(name, src_low, dst_high, -distance, 0),
            send(name, src_high, dst_low, distance, 1),
        )
        for copy in copies:
            copy.start()
        pending[name] = copies

    def arrived(*names):
        for name in names:
            for copy in pending[name]:
                copy.wait_recv()

    def sent(*names):
        for name in names:
            for copy in pending.pop(name):
                copy.wait_send()

    def scales(level, lo, hi):
        top = relax_weight * (damping + nominal_stiff / 4.0**level)
        def fn(at):
            for i in at:
                S[level][i] = top / (damping + 4.0 * K[level][i])
        rows(lo, hi, 24, fn)

    def relax(level, lo, hi, d_ref):
        def fn(at):
            for i in at:
                d_ref[i] = columns(w_ref[level], S[level][i] * R[level][i])
        rows(lo, hi, 24, fn)

    def update(level, lo, hi, d_ref):
        shift = nominal_stiff / 4.0**level
        def fn(at):
            for i in at:
                d = d_ref[i]
                beside_sum = d_ref[i - 1] + d_ref[i + 1] + lateral(d, masked(level))
                t = S[level][i] * R[level][i]
                R[level][i] = R[level][i] - t + shift * d + K[level][i] * (beside_sum - 4.0 * d)
        rows(lo, hi, 24, fn)

    def lift(level, lo, hi, e_ref, v_ref):
        def fn(at):
            for i in at:
                e = e_ref[i]
                beside_sum = e_ref[i - 1] + e_ref[i + 1] + lateral(e, masked(level))
                R[level][i] = R[level][i] - v_ref[i] + K[level][i] * (beside_sum - 4.0 * e)
        rows(lo, hi, 24, fn)

    def coarsen(level, src, dst, scale, which=None):
        matrix = coarse0_ref if level == 0 else coarse_ref
        def fn(at):
            for j in at:
                fine = H[level] + 2 * j
                dst[H[level + 1] + j] = lanes(scale * (src[fine] + src[fine + 1]), matrix[...])
        fn(range(own[level + 1]) if which is None else which)

    def refine(level, lo, hi, src, e_ref, v_ref):
        matrix = fine0_ref if level == 0 else fine_ref
        def fn(at):
            for j in at:
                e = src[j]
                to = H[level] + 2 * (j - H[level + 1])
                value = lanes(e, matrix[...])
                product = lanes(columns(wv_ref[...], e), matrix[...])
                for i in (to, to + 1):
                    e_ref[i] = value
                    v_ref[i] = product
        rows(lo, hi, 24, fn)

    zero = jnp.zeros((LEV, 256), F32)
    p0[0] = zero
    p0[17] = zero
    pltpu.make_async_copy(p0.at[pl.ds(1, 16)], p0.at[pl.ds(1, 16)], in_sem.at[0]).wait()
    pltpu.make_async_copy(k0.at[pl.ds(4, 16)], k0.at[pl.ds(4, 16)], in_sem.at[1]).wait()
    pltpu.make_async_copy(r0.at[pl.ds(4, 16)], r0.at[pl.ds(4, 16)], in_sem.at[2]).wait()

    def start(at):
        for i in at:
            x = p0[i + 1]
            beside_sum = p0[i] + p0[i + 2] + lateral(x, True)
            r0[i + 4] = r0[i + 4] - columns(wv_ref[...], x) + k0[i + 4] * (beside_sum - 4.0 * x)
    rows(0, 16, 24, start)
    dh[2] = r0[4]
    dh[3] = r0[19]

    pl.semaphore_wait(barrier, 6)
    exchange("p", p0.at[1], ph.at[0], p0.at[16], ph.at[1])
    exchange("k", k0.at[4], k0.at[3], k0.at[19], k0.at[20])
    exchange("r", dh.at[2], rh.at[0], dh.at[3], rh.at[1])

    for level in range(LEVELS - 1):
        coarsen(level, K[level], K[level + 1], 1.0 / 16.0)
    exchange("k1", k1.at[pl.ds(4, 3)], k1.at[pl.ds(1, 3)], k1.at[pl.ds(9, 3)], k1.at[pl.ds(12, 3)])
    q2[6] = pack2(k2[4], k2[5])
    q2[7] = pack2(k2[6], k2[7])
    exchange("k2", q2.at[pl.ds(6, 2)], lk2.at[pl.ds(0, 2)], q2.at[pl.ds(6, 2)], lk2.at[pl.ds(2, 2)])

    scales(0, 4, 20)
    relax(0, 5, 19, da0)
    update(0, 6, 18, da0)
    relax(0, 6, 18, db0)
    db0[3] = zero
    db0[20] = zero
    update(0, 7, 17, db0)
    coarsen(0, r0, r1, 0.25, (2, 3, 4, 5))
    scales(1, 4, 12)
    scales(2, 4, 8)
    scales(3, 5, 7)

    arrived("p", "k", "r")
    for side, edge, halo in ((0, 4, 3), (1, 19, 20)):
        r0[halo] = rh[side] + k0[halo] * p0[edge - 3]
        r0[edge] = r0[edge] + k0[edge] * ph[side]
        scales(0, halo, halo + 1)
    for lo, hi in ((3, 5), (19, 21)):
        relax(0, lo, hi, da0)
    for lo, hi in ((4, 6), (18, 20)):
        update(0, lo, hi, da0)
    for lo, hi in ((4, 6), (18, 20)):
        relax(0, lo, hi, db0)
    exchange("d", db0.at[4], dh.at[0], db0.at[19], dh.at[1])
    for lo, hi in ((4, 7), (17, 20)):
        update(0, lo, hi, db0)
    coarsen(0, r0, r1, 0.25, (0, 1, 6, 7))
    for n, i in enumerate((4, 5, 10, 11)):
        lr1[6 + n] = r1[i]
    for n, i in enumerate((4, 5, 18, 19)):
        lr0[4 + n] = r0[i]
    exchange("b1", lr1.at[pl.ds(6, 2)], r1.at[pl.ds(2, 2)], lr1.at[pl.ds(8, 2)], r1.at[pl.ds(12, 2)])
    exchange("r0", lr0.at[pl.ds(4, 2)], lr0.at[pl.ds(0, 2)], lr0.at[pl.ds(6, 2)], lr0.at[pl.ds(2, 2)])

    spread3("k3", 0, k3)

    def gather(at):
        for i in at:
            c0[i - 4] = p0[i - 3] + da0[i] + db0[i]
    rows(4, 20, 24, gather)
    arrived("k1", "k2")
    for n in range(4):
        k2[(0, 2, 8, 10)[n]], k2[(1, 3, 9, 11)[n]] = unpack2(lk2[n])
    for lo, hi in ((1, 4), (12, 15)):
        scales(1, lo, hi)
    for lo, hi in ((1, 4), (8, 11)):
        scales(2, lo, hi)

    arrived("d", "b1")
    for side, edge, halo, edge1, halo1 in ((0, 4, 3, 4, 3), (1, 19, 20, 11, 12)):
        mine = k0[edge] * dh[side]
        theirs = k0[halo] * db0[edge]
        r0[edge] = r0[edge] + mine
        dh[4 + side] = theirs
        r1[edge1] = r1[edge1] + lanes(0.25 * mine, coarse0_ref[...])
        r1[halo1] = r1[halo1] + lanes(0.25 * theirs, coarse0_ref[...])

    relax(1, 2, 14, da1)
    update(1, 3, 13, da1)
    relax(1, 3, 13, db1)
    update(1, 4, 12, db1)
    coarsen(1, r1, r2, 0.25)
    q2[4] = pack2(r2[4], r2[5])
    q2[5] = pack2(r2[6], r2[7])
    exchange("b2", q2.at[4], lb2.at[0], q2.at[5], lb2.at[1])
    for n, i in enumerate((5, 10)):
        lc1[2 + n] = db1[i]
    exchange("c1", lc1.at[2], lc1.at[0], lc1.at[3], lc1.at[1])
    exchange("r1", r1.at[pl.ds(5, 2)], lr1.at[pl.ds(0, 2)], r1.at[pl.ds(9, 2)], lr1.at[pl.ds(2, 2)])
    for i in range(3, 13):
        c1[i] = da1[i] + db1[i]

    exchange("k_far", k0.at[5], k0.at[2], k0.at[18], k0.at[21])

    arrived("r0")
    r0[2] = lr0[0]
    r0[3] = lr0[1] + dh[4]
    r0[20] = lr0[2] + dh[5]
    r0[21] = lr0[3]

    arrived("b2")
    r2[2], r2[3] = unpack2(lb2[0])
    r2[8], r2[9] = unpack2(lb2[1])
    relax(2, 2, 10, da2)
    update(2, 3, 9, da2)
    relax(2, 3, 9, db2)
    update(2, 4, 8, db2)
    coarsen(2, r2, r3, 0.25)
    spread3("b3", 1, r3)
    q2[0] = pack2(r2[5], r2[6])
    q2[1] = pack2(db2[5], db2[6])
    exchange("r2", q2.at[pl.ds(0, 2)], lr2.at[pl.ds(0, 2)], q2.at[pl.ds(0, 2)], lr2.at[pl.ds(2, 2)])
    for i in range(3, 9):
        c2[i] = da2[i] + db2[i]
    arrived("k3", "k3_2", "k3_3")
    gather3(0, k3)
    for lo, hi in ((0, 5), (7, 12)):
        scales(3, lo, hi)

    arrived("b3", "b3_2", "b3_3")
    gather3(1, r3)
    relax(3, 0, 12, da3)
    update(3, 1, 11, da3)
    relax(3, 1, 11, db3)
    update(3, 2, 10, db3)
    def first(at):
        for i in at:
            c3[i] = da3[i] + db3[i]
    rows(3, 9, 24, first)
    relax(3, 2, 10, da3)
    update(3, 3, 9, da3)
    relax(3, 3, 9, db3)
    def last(at):
        for i in at:
            c3[i] = c3[i] + da3[i] + db3[i]
    rows(3, 9, 24, last)

    refine(2, 3, 9, c3, e2, v2)
    arrived("r2")
    db2[2] = unpack2(lr2[1])[1]
    db2[9] = unpack2(lr2[3])[0]
    update(2, 3, 4, db2)
    update(2, 8, 9, db2)
    r2[1], r2[2] = unpack2(lr2[0])
    r2[9], r2[10] = unpack2(lr2[2])
    for i in (2, 9):
        c2[i] = da2[i] + db2[i]
    lift(2, 1, 11, e2, v2)
    relax(2, 1, 11, da2)
    update(2, 2, 10, da2)
    relax(2, 2, 10, db2)
    def sum2(at):
        for i in at:
            c2[i] = c2[i] + e2[i] + da2[i] + db2[i]
    rows(2, 10, 24, sum2)

    refine(1, 2, 10, c2, e1, v1)
    arrived("r1", "c1")
    sent("r1", "c1")
    for n, i in enumerate((2, 13)):
        db1[i] = lc1[n]
    update(1, 3, 4, db1)
    update(1, 12, 13, db1)
    for n, i in enumerate((1, 2, 13, 14)):
        r1[i] = lr1[n]
    for n, i in enumerate((2, 13)):
        c1[i] = da1[i] + lc1[n]
    lift(1, 1, 15, e1, v1)
    relax(1, 1, 15, da1)
    update(1, 2, 14, da1)
    relax(1, 2, 14, db1)
    def sum1(at):
        for i in at:
            c1[i] = c1[i] + e1[i] + da1[i] + db1[i]
    rows(2, 14, 24, sum1)

    arrived("k_far")
    for lo, hi in ((2, 3), (21, 22)):
        scales(0, lo, hi)
    refine(0, 2, 14, c1, e0, v0)
    sent("d")
    lift(0, 2, 22, e0, v0)
    relax(0, 2, 22, da0)
    update(0, 3, 21, da0)
    relax(0, 3, 21, db0)
    def sum0(at):
        for i in at:
            c0[i - 4] = c0[i - 4] + e0[i] + da0[i] + db0[i]
    rows(4, 20, 24, sum0)
    for i in range(16):
        pltpu.make_async_copy(c0.at[i], out_u.at[:, i, :], out_sem.at[0]).start()
    update(0, 4, 20, db0)
    for i in range(16):
        pltpu.make_async_copy(r0.at[4 + i], out_r.at[:, i, :], out_sem.at[1]).start()
    sent(*list(pending))
    pltpu.make_async_copy(c0, c0, out_sem.at[0]).wait()
    pltpu.make_async_copy(r0.at[pl.ds(4, 16)], r0.at[pl.ds(4, 16)], out_sem.at[1]).wait()


def solution(mesh):
    faces, tiles = mesh.shape["face"], mesh.shape["tile"]

    def field(count, width):
        return pltpu.VMEM((count, LEV, width), F32)

    def body(pressure, forcing, stiffness, vertical_op, col_inverse):
        out = jax.ShapeDtypeStruct(pressure.shape, F32)
        def level(n, extra):
            return [field(n, LANES)] * 8 + [field(m, LANES) for m in extra]
        scratch = (
            [field(18, 256)] + [field(24, 256)] * 7 + [field(2, 256)] * 2 + [field(6, 256), field(8, 256)]
            + level(16, (10, 4)) + level(12, (6, 2))
            + [field(12, LANES)] * 6 + [field(16, 256), field(4, LANES), field(8, LANES)]
            + [pltpu.VMEM((2, LEV // 2, LANES), F32), pltpu.VMEM((12, LEV // 2, LANES), F32)]
            + [pltpu.VMEM((8, LEV // 4, LANES), F32)]
            + [
                pltpu.VMEM((LEVELS, LEV, 3 * LEV), BF16),
                pltpu.VMEM((LEV, 3 * LEV), BF16),
                pltpu.VMEM((256, 128), BF16),
                pltpu.VMEM((512, 128), BF16),
                pltpu.VMEM((256, 128), BF16),
                pltpu.VMEM((256, 256), BF16),
                pltpu.SemaphoreType.DMA((3,)),
                pltpu.SemaphoreType.DMA((2,)),
                pltpu.SemaphoreType.DMA((len(MESSAGES), 2)),
                pltpu.SemaphoreType.DMA((len(MESSAGES), 2)),
            ]
        )
        return pl.pallas_call(
            functools.partial(kernel, faces, tiles),
            out_shape=(out, out),
            in_specs=[pl.BlockSpec(memory_space=pl.ANY)] * 3 + [pl.BlockSpec(memory_space=pltpu.VMEM)] * 2,
            out_specs=(pl.BlockSpec(memory_space=pl.ANY),) * 2,
            scratch_shapes=scratch,
            compiler_params=pltpu.CompilerParams(
                collective_id=0, has_side_effects=True, vmem_limit_bytes=VMEM_MIB * 1024 * 1024
            ),
            cost_estimate=pl.CostEstimate(flops=2_000_000_000, bytes_accessed=5_000_000, transcendentals=0),
        )(pressure, forcing, stiffness, vertical_op, col_inverse)

    belt = P(None, ("face", "tile"), None)
    return jax.shard_map(
        body,
        mesh=mesh,
        in_specs=(belt, belt, belt, P(), P()),
        out_specs=(belt, belt),
        check_vma=False,
    )
```

```python
import functools

import jax
import jax.numpy as jnp
from jax import lax
from jax.experimental import pallas as pl
from jax.experimental.pallas import tpu as pltpu
from jax.sharding import PartitionSpec as P

LEVELS = 4
LEV = 64
damping = 0.02
relax_weight = 0.6
nominal_stiff = 16.0
F32, BF16 = jnp.float32, jnp.bfloat16
MESH = pl.DeviceIdType.MESH
LANES = 128
VMEM_MIB = 62

HALO = (4, 4, 4, 5)

MESSAGES = (
    "p", "k", "r", "k_far", "k1", "k2", "k3", "k3_2", "k3_3", "d", "b1", "r0", "b2", "r1", "c1",
    "b3", "b3_2", "b3_3", "r2",
)


def split(x):
    high = x.astype(BF16)
    return high, (x - high.astype(F32)).astype(BF16)


def rows(lo, hi, step, fn):
    whole, rest = divmod(hi - lo, step)
    if whole > 1:
        def body(i, carry):
            base = lo + i * step
            fn([base + j for j in range(step)])
            return carry
        lax.fori_loop(0, whole, body, 0)
    elif whole == 1:
        fn([lo + j for j in range(step)])
    if rest:
        fn([hi - rest + j for j in range(rest)])


def lateral(x, masked):
    width = x.shape[1]
    below, above = pltpu.roll(x, 1, 1), pltpu.roll(x, width - 1, 1)
    if masked:
        lane = lax.broadcasted_iota(jnp.int32, x.shape, 1)
        below = jnp.where(lane == 0, 0.0, below)
        above = jnp.where(lane == width - 1, 0.0, above)
    return below + above


def kernel(
    faces, tiles, p_hbm, f_hbm, k_hbm, vop_ref, inv_ref, out_u, out_r,
    p0, k0, s0, r0, da0, db0, e0, v0, ph, rh, dh, lr0,
    k1, s1, r1, da1, db1, c1, e1, v1, lr1, lc1,
    k2, s2, r2, da2, db2, c2, e2, v2, lr2, lb2,
    k3, s3, r3, da3, db3, c3, c0, lk2, q2, q3, lq3, q4,
    w_ref, wv_ref, coarse_ref, coarse0_ref, fine_ref, fine0_ref,
    in_sem, out_sem, send_sem, recv_sem,
):
    count = faces * tiles
    me = lax.axis_index("face") * tiles + lax.axis_index("tile")

    def device(offset):
        other = lax.rem(me + (offset + count), count)
        return (other // tiles, lax.rem(other, tiles))

    barrier = pltpu.get_barrier_semaphore()
    for offset in (-3, -2, -1, 1, 2, 3):
        pl.semaphore_signal(barrier, inc=1, device_id=device(offset), device_id_type=MESH)

    K, S, R, DA, DB = (k0, k1, k2, k3), (s0, s1, s2, s3), (r0, r1, r2, r3), (da0, da1, da2, da3), (db0, db1, db2, db3)
    C = (c0, c1, c2, c3)
    own = tuple(n_rows >> level for level, n_rows in enumerate((16,) * LEVELS))
    H = HALO

    for i in range(16):
        pltpu.make_async_copy(p_hbm.at[:, i, :], p0.at[1 + i], in_sem.at[0]).start()
    for i in range(16):
        pltpu.make_async_copy(k_hbm.at[:, i, :], k0.at[H[0] + i], in_sem.at[1]).start()
    for i in range(16):
        pltpu.make_async_copy(f_hbm.at[:, i, :], r0.at[H[0] + i], in_sem.at[2]).start()

    def beside(m):
        high, low = split(m)
        return jnp.concatenate([high, high, low], axis=1)

    for level in range(LEVELS):
        w_ref[level] = beside(inv_ref[level])
    row, col = (lax.broadcasted_iota(jnp.int32, (LEV, LEV), a) for a in (0, 1))
    wv_ref[...] = beside(vop_ref[...] + jnp.where(row == col, damping, 0.0))

    def pairs(n_in, n_out, fold):
        a, b = (lax.broadcasted_iota(jnp.int32, (2 * n_in, n_out), x) for x in (0, 1))
        a = jnp.where(a >= n_in, a - n_in, a)
        hit = (a // 2 == b) if fold else (a == b // 2)
        return jnp.where(hit, 1.0, 0.0).astype(BF16)

    coarse0_ref[...] = pairs(256, 128, True)
    coarse_ref[...] = pairs(128, 128, True)
    fine0_ref[...] = pairs(128, 256, False)
    fine_ref[...] = pairs(128, 128, False)

    def stacked(x):
        high, low = split(x)
        return jnp.concatenate([high, low, high], axis=0)

    def columns(w, x):
        return jnp.dot(w, stacked(x), preferred_element_type=F32)

    def lanes(x, matrix):
        high, low = split(x)
        return jnp.dot(jnp.concatenate([high, low], axis=1), matrix, preferred_element_type=F32)

    def lane_mask(x, lo, hi):
        lane = lax.broadcasted_iota(jnp.int32, x.shape, 1)
        return jnp.where((lane >= lo) & (lane < hi), x, 0.0)

    def pack2(a, b):
        return a + pltpu.roll(b, 64, 1)

    def unpack2(x):
        return lane_mask(x, 0, 64), lane_mask(pltpu.roll(x, 64, 1), 0, 64)

    def pack3(a, b):
        both = a + pltpu.roll(b, 32, 1)
        half = LEV // 2
        return both[:half] + pltpu.roll(both[half:], 64, 1)

    def unpack3(x):
        parts = [x] + [pltpu.roll(x, shift, 1) for shift in (64, 96, 32)]
        parts = [lane_mask(part, 0, 32) for part in parts]
        return jnp.concatenate(parts[:2], axis=0), jnp.concatenate(parts[2:], axis=0)

    def pack4(x):
        quarter = LEV // 4
        parts = [x[n * quarter : (n + 1) * quarter] for n in range(4)]
        return sum(pltpu.roll(part, 32 * n, 1) for n, part in enumerate(parts[1:], 1)) + parts[0]

    def unpack4(x):
        parts = [x] + [pltpu.roll(x, LANES - 32 * n, 1) for n in (1, 2, 3)]
        return jnp.concatenate([lane_mask(part, 0, 32) for part in parts], axis=0)

    def spread3(name, at, src):
        q3[at] = pack3(src[5], src[6])
        q4[2 * at] = pack4(src[5])
        q4[2 * at + 1] = pack4(src[6])
        for distance in (1, 2):
            low, high = at * 6 + 3 - distance, at * 6 + 2 + distance
            suffix = "" if distance == 1 else "_%d" % distance
            exchange(name + suffix, q3.at[at], lq3.at[low], q3.at[at], lq3.at[high], distance)
        first_in, last_in = 4 + 2 * at, 5 + 2 * at
        exchange(name + "_3", q4.at[2 * at], q4.at[first_in], q4.at[2 * at + 1], q4.at[last_in], 3)

    def gather3(at, to):
        for n, i in ((1, 1), (2, 3), (3, 7), (4, 9)):
            to[i], to[i + 1] = unpack3(lq3[at * 6 + n])
        to[0] = unpack4(q4[4 + 2 * at])
        to[11] = unpack4(q4[5 + 2 * at])

    def masked(level):
        return level < 2

    def send(name, src, dst, offset, side):
        at = MESSAGES.index(name)
        return pltpu.make_async_remote_copy(
            src_ref=src, dst_ref=dst, send_sem=send_sem.at[at, side], recv_sem=recv_sem.at[at, side],
            device_id=device(offset), device_id_type=MESH,
        )

    pending = {}

    def exchange(name, src_low, dst_low, src_high, dst_high, distance=1):
        copies = (
            send(name, src_low, dst_high, -distance, 0),
            send(name, src_high, dst_low, distance, 1),
        )
        for copy in copies:
            copy.start()
        pending[name] = copies

    def arrived(*names):
        for name in names:
            for copy in pending[name]:
                copy.wait_recv()

    def sent(*names):
        for name in names:
            for copy in pending.pop(name):
                copy.wait_send()

    def scales(level, lo, hi):
        top = relax_weight * (damping + nominal_stiff / 4.0**level)
        def fn(at):
            for i in at:
                S[level][i] = top / (damping + 4.0 * K[level][i])
        rows(lo, hi, 24, fn)

    def relax(level, lo, hi, d_ref):
        def fn(at):
            for i in at:
                d_ref[i] = columns(w_ref[level], S[level][i] * R[level][i])
        rows(lo, hi, 24, fn)

    def update(level, lo, hi, d_ref):
        shift = nominal_stiff / 4.0**level
        def fn(at):
            for i in at:
                d = d_ref[i]
                beside_sum = d_ref[i - 1] + d_ref[i + 1] + lateral(d, masked(level))
                t = S[level][i] * R[level][i]
                R[level][i] = R[level][i] - t + shift * d + K[level][i] * (beside_sum - 4.0 * d)
        rows(lo, hi, 24, fn)

    def lift(level, lo, hi, e_ref, v_ref):
        def fn(at):
            for i in at:
                e = e_ref[i]
                beside_sum = e_ref[i - 1] + e_ref[i + 1] + lateral(e, masked(level))
                R[level][i] = R[level][i] - v_ref[i] + K[level][i] * (beside_sum - 4.0 * e)
        rows(lo, hi, 24, fn)

    def coarsen(level, src, dst, scale, which=None):
        matrix = coarse0_ref if level == 0 else coarse_ref
        def fn(at):
            for j in at:
                fine = H[level] + 2 * j
                dst[H[level + 1] + j] = lanes(scale * (src[fine] + src[fine + 1]), matrix[...])
        fn(range(own[level + 1]) if which is None else which)

    def refine(level, lo, hi, src, e_ref, v_ref):
        matrix = fine0_ref if level == 0 else fine_ref
        def fn(at):
            for j in at:
                e = src[j]
                to = H[level] + 2 * (j - H[level + 1])
                value = lanes(e, matrix[...])
                product = lanes(columns(wv_ref[...], e), matrix[...])
                for i in (to, to + 1):
                    e_ref[i] = value
                    v_ref[i] = product
        rows(lo, hi, 24, fn)

    zero = jnp.zeros((LEV, 256), F32)
    p0[0] = zero
    p0[17] = zero
    pltpu.make_async_copy(p0.at[pl.ds(1, 16)], p0.at[pl.ds(1, 16)], in_sem.at[0]).wait()
    pltpu.make_async_copy(k0.at[pl.ds(4, 16)], k0.at[pl.ds(4, 16)], in_sem.at[1]).wait()
    pltpu.make_async_copy(r0.at[pl.ds(4, 16)], r0.at[pl.ds(4, 16)], in_sem.at[2]).wait()

    def start(at):
        for i in at:
            x = p0[i + 1]
            beside_sum = p0[i] + p0[i + 2] + lateral(x, True)
            r0[i + 4] = r0[i + 4] - columns(wv_ref[...], x) + k0[i + 4] * (beside_sum - 4.0 * x)
    rows(0, 16, 24, start)
    dh[2] = r0[4]
    dh[3] = r0[19]

    pl.semaphore_wait(barrier, 6)
    exchange("p", p0.at[1], ph.at[0], p0.at[16], ph.at[1])
    exchange("k", k0.at[4], k0.at[3], k0.at[19], k0.at[20])
    exchange("r", dh.at[2], rh.at[0], dh.at[3], rh.at[1])

    for level in range(LEVELS - 1):
        coarsen(level, K[level], K[level + 1], 1.0 / 16.0)
    exchange("k1", k1.at[pl.ds(4, 3)], k1.at[pl.ds(1, 3)], k1.at[pl.ds(9, 3)], k1.at[pl.ds(12, 3)])
    q2[6] = pack2(k2[4], k2[5])
    q2[7] = pack2(k2[6], k2[7])
    exchange("k2", q2.at[pl.ds(6, 2)], lk2.at[pl.ds(0, 2)], q2.at[pl.ds(6, 2)], lk2.at[pl.ds(2, 2)])

    scales(0, 4, 20)
    relax(0, 5, 19, da0)
    update(0, 6, 18, da0)
    relax(0, 6, 18, db0)
    db0[3] = zero
    db0[20] = zero
    update(0, 7, 17, db0)
    coarsen(0, r0, r1, 0.25, (2, 3, 4, 5))
    scales(1, 4, 12)
    scales(2, 4, 8)
    scales(3, 5, 7)

    arrived("p", "k", "r")
    for side, edge, halo in ((0, 4, 3), (1, 19, 20)):
        r0[halo] = rh[side] + k0[halo] * p0[edge - 3]
        r0[edge] = r0[edge] + k0[edge] * ph[side]
        scales(0, halo, halo + 1)
    for lo, hi in ((3, 5), (19, 21)):
        relax(0, lo, hi, da0)
    for lo, hi in ((4, 6), (18, 20)):
        update(0, lo, hi, da0)
    for lo, hi in ((4, 6), (18, 20)):
        relax(0, lo, hi, db0)
    exchange("d", db0.at[4], dh.at[0], db0.at[19], dh.at[1])
    for lo, hi in ((4, 7), (17, 20)):
        update(0, lo, hi, db0)
    coarsen(0, r0, r1, 0.25, (0, 1, 6, 7))
    for n, i in enumerate((4, 5, 10, 11)):
        lr1[6 + n] = r1[i]
    for n, i in enumerate((4, 5, 18, 19)):
        lr0[4 + n] = r0[i]
    exchange("b1", lr1.at[pl.ds(6, 2)], r1.at[pl.ds(2, 2)], lr1.at[pl.ds(8, 2)], r1.at[pl.ds(12, 2)])
    exchange("r0", lr0.at[pl.ds(4, 2)], lr0.at[pl.ds(0, 2)], lr0.at[pl.ds(6, 2)], lr0.at[pl.ds(2, 2)])

    spread3("k3", 0, k3)

    def gather(at):
        for i in at:
            c0[i - 4] = p0[i - 3] + da0[i] + db0[i]
    rows(4, 20, 24, gather)
    arrived("k1", "k2")
    for n in range(4):
        k2[(0, 2, 8, 10)[n]], k2[(1, 3, 9, 11)[n]] = unpack2(lk2[n])
    for lo, hi in ((1, 4), (12, 15)):
        scales(1, lo, hi)
    for lo, hi in ((1, 4), (8, 11)):
        scales(2, lo, hi)

    arrived("d", "b1")
    for side, edge, halo, edge1, halo1 in ((0, 4, 3, 4, 3), (1, 19, 20, 11, 12)):
        mine = k0[edge] * dh[side]
        theirs = k0[halo] * db0[edge]
        r0[edge] = r0[edge] + mine
        dh[4 + side] = theirs
        r1[edge1] = r1[edge1] + lanes(0.25 * mine, coarse0_ref[...])
        r1[halo1] = r1[halo1] + lanes(0.25 * theirs, coarse0_ref[...])

    relax(1, 2, 14, da1)
    update(1, 3, 13, da1)
    relax(1, 3, 13, db1)
    update(1, 4, 12, db1)
    coarsen(1, r1, r2, 0.25)
    q2[4] = pack2(r2[4], r2[5])
    q2[5] = pack2(r2[6], r2[7])
    exchange("b2", q2.at[4], lb2.at[0], q2.at[5], lb2.at[1])
    for n, i in enumerate((5, 10)):
        lc1[2 + n] = db1[i]
    exchange("c1", lc1.at[2], lc1.at[0], lc1.at[3], lc1.at[1])
    exchange("r1", r1.at[pl.ds(5, 2)], lr1.at[pl.ds(0, 2)], r1.at[pl.ds(9, 2)], lr1.at[pl.ds(2, 2)])
    for i in range(3, 13):
        c1[i] = da1[i] + db1[i]


    arrived("r0")
    r0[2] = lr0[0]
    r0[3] = lr0[1] + dh[4]
    r0[20] = lr0[2] + dh[5]
    r0[21] = lr0[3]

    arrived("b2")
    r2[2], r2[3] = unpack2(lb2[0])
    r2[8], r2[9] = unpack2(lb2[1])
    relax(2, 2, 10, da2)
    update(2, 3, 9, da2)
    relax(2, 3, 9, db2)
    update(2, 4, 8, db2)
    coarsen(2, r2, r3, 0.25)
    spread3("b3", 1, r3)
    q2[0] = pack2(r2[5], r2[6])
    q2[1] = pack2(db2[5], db2[6])
    exchange("r2", q2.at[pl.ds(0, 2)], lr2.at[pl.ds(0, 2)], q2.at[pl.ds(0, 2)], lr2.at[pl.ds(2, 2)])
    exchange("k_far", k0.at[5], k0.at[2], k0.at[18], k0.at[21])
    for i in range(3, 9):
        c2[i] = da2[i] + db2[i]
    arrived("k3", "k3_2", "k3_3")
    gather3(0, k3)
    for lo, hi in ((0, 5), (7, 12)):
        scales(3, lo, hi)

    arrived("b3", "b3_2", "b3_3")
    gather3(1, r3)
    relax(3, 0, 12, da3)
    update(3, 1, 11, da3)
    relax(3, 1, 11, db3)
    update(3, 2, 10, db3)
    def first(at):
        for i in at:
            c3[i] = da3[i] + db3[i]
    rows(3, 9, 24, first)
    relax(3, 2, 10, da3)
    update(3, 3, 9, da3)
    relax(3, 3, 9, db3)
    def last(at):
        for i in at:
            c3[i] = c3[i] + da3[i] + db3[i]
    rows(3, 9, 24, last)

    refine(2, 3, 9, c3, e2, v2)
    arrived("r2")
    db2[2] = unpack2(lr2[1])[1]
    db2[9] = unpack2(lr2[3])[0]
    update(2, 3, 4, db2)
    update(2, 8, 9, db2)
    r2[1], r2[2] = unpack2(lr2[0])
    r2[9], r2[10] = unpack2(lr2[2])
    for i in (2, 9):
        c2[i] = da2[i] + db2[i]
    lift(2, 1, 11, e2, v2)
    relax(2, 1, 11, da2)
    update(2, 2, 10, da2)
    relax(2, 2, 10, db2)
    def sum2(at):
        for i in at:
            c2[i] = c2[i] + e2[i] + da2[i] + db2[i]
    rows(2, 10, 24, sum2)

    refine(1, 2, 10, c2, e1, v1)
    arrived("r1", "c1")
    sent("r1", "c1")
    for n, i in enumerate((2, 13)):
        db1[i] = lc1[n]
    update(1, 3, 4, db1)
    update(1, 12, 13, db1)
    for n, i in enumerate((1, 2, 13, 14)):
        r1[i] = lr1[n]
    for n, i in enumerate((2, 13)):
        c1[i] = da1[i] + lc1[n]
    lift(1, 1, 15, e1, v1)
    relax(1, 1, 15, da1)
    update(1, 2, 14, da1)
    relax(1, 2, 14, db1)
    def sum1(at):
        for i in at:
            c1[i] = c1[i] + e1[i] + da1[i] + db1[i]
    rows(2, 14, 24, sum1)

    arrived("k_far")
    for lo, hi in ((2, 3), (21, 22)):
        scales(0, lo, hi)
    refine(0, 2, 14, c1, e0, v0)
    sent("d")
    lift(0, 2, 22, e0, v0)
    relax(0, 2, 22, da0)
    update(0, 3, 21, da0)
    relax(0, 3, 21, db0)
    def sum0(at):
        for i in at:
            c0[i - 4] = c0[i - 4] + e0[i] + da0[i] + db0[i]
    rows(4, 20, 24, sum0)
    for i in range(16):
        pltpu.make_async_copy(c0.at[i], out_u.at[:, i, :], out_sem.at[0]).start()
    update(0, 4, 20, db0)
    for i in range(16):
        pltpu.make_async_copy(r0.at[4 + i], out_r.at[:, i, :], out_sem.at[1]).start()
    sent(*list(pending))
    pltpu.make_async_copy(c0, c0, out_sem.at[0]).wait()
    pltpu.make_async_copy(r0.at[pl.ds(4, 16)], r0.at[pl.ds(4, 16)], out_sem.at[1]).wait()


def solution(mesh):
    faces, tiles = mesh.shape["face"], mesh.shape["tile"]

    def field(count, width):
        return pltpu.VMEM((count, LEV, width), F32)

    def body(pressure, forcing, stiffness, vertical_op, col_inverse):
        out = jax.ShapeDtypeStruct(pressure.shape, F32)
        def level(n, extra):
            return [field(n, LANES)] * 8 + [field(m, LANES) for m in extra]
        scratch = (
            [field(18, 256)] + [field(24, 256)] * 7 + [field(2, 256)] * 2 + [field(6, 256), field(8, 256)]
            + level(16, (10, 4)) + level(12, (6, 2))
            + [field(12, LANES)] * 6 + [field(16, 256), field(4, LANES), field(8, LANES)]
            + [pltpu.VMEM((2, LEV // 2, LANES), F32), pltpu.VMEM((12, LEV // 2, LANES), F32)]
            + [pltpu.VMEM((8, LEV // 4, LANES), F32)]
            + [
                pltpu.VMEM((LEVELS, LEV, 3 * LEV), BF16),
                pltpu.VMEM((LEV, 3 * LEV), BF16),
                pltpu.VMEM((256, 128), BF16),
                pltpu.VMEM((512, 128), BF16),
                pltpu.VMEM((256, 128), BF16),
                pltpu.VMEM((256, 256), BF16),
                pltpu.SemaphoreType.DMA((3,)),
                pltpu.SemaphoreType.DMA((2,)),
                pltpu.SemaphoreType.DMA((len(MESSAGES), 2)),
                pltpu.SemaphoreType.DMA((len(MESSAGES), 2)),
            ]
        )
        return pl.pallas_call(
            functools.partial(kernel, faces, tiles),
            out_shape=(out, out),
            in_specs=[pl.BlockSpec(memory_space=pl.ANY)] * 3 + [pl.BlockSpec(memory_space=pltpu.VMEM)] * 2,
            out_specs=(pl.BlockSpec(memory_space=pl.ANY),) * 2,
            scratch_shapes=scratch,
            compiler_params=pltpu.CompilerParams(
                collective_id=0, has_side_effects=True, vmem_limit_bytes=VMEM_MIB * 1024 * 1024
            ),
            cost_estimate=pl.CostEstimate(flops=2_000_000_000, bytes_accessed=5_000_000, transcendentals=0),
        )(pressure, forcing, stiffness, vertical_op, col_inverse)

    belt = P(None, ("face", "tile"), None)
    return jax.shard_map(
        body,
        mesh=mesh,
        in_specs=(belt, belt, belt, P(), P()),
        out_specs=(belt, belt),
        check_vma=False,
    )
```
